32 devices in a mesh: grp: 2 (over x), dom: 4 (over y, core), test: 4 (over z).
Axes of the slice: x: 2, y: 2, z: 4, core: 2. Of those that a mesh axis runs over, the one named last changes fastest.
Arguments:
- log_conductivity: float32 [16, 32, 512], P('grp', 'dom'), parts along dimension 0, may hold values from -3 to 3
- storage: float32 [16, 32, 512], P('grp', 'dom'), parts along dimension 0, may hold values from 0.05 to 0.5
- recharge: float32 [16, 32, 512], P('grp', 'dom'), parts along dimension 0, may hold values from -4 to 4
- pump_cells: int32 [8], P(('grp', 'test')), parts along dimension 0, may hold values from 0 to 131071
- obs_cells: int32 [8, 32], P(('grp', 'test')), parts along dimension 0, may hold values from 0 to 131071
- obs_heads: float32 [8, 32], P(('grp', 'test')), parts along dimension 0, may hold values from -4 to 4
Outputs:
- gradient: float32 [16, 32, 512], P(('grp', 'test'), 'dom'), parts along dimension 0
- step_field: float32 [16, 32, 512], P(('grp', 'test'), 'dom'), parts along dimension 0
The draws below stay inside these ranges and needn't reach their ends.
There are 2 independent parts, one for each index of `grp`. The reference program is written for one: setup_inputs(seed, part) draws one part's arguments, and reference() takes and returns one part's arrays. A program takes and returns all parts, laid end to end along the dimension named above; each array names one. Nothing has to cross between parts.
Inputs may be any that keep to these rules, and one draw needn't show every extreme that they name: `pump_cells`: flat index 32 * 512 * z + 512 * x + y of the pumping well's cell. `obs_cells`: flat index 32 * 512 * z + 512 * x + y of each port's cell; ports may repeat.
All inputs are finite; a program needn't handle non-finite values.
Results may differ from the reference program's by a relative error of at most 0.00027.
Values sent between devices are 32-bit elements; how exact they have to be, the bound alone decides.
A program may use at most 64 MiB of HBM per device.

```python
import math
import jax
import jax.numpy as jnp
from jax import lax

NY = 512
NZ = 8
OBS = 32
ITERS = 32
NX = 32
TESTS = 4
CORR = 16


def draw_recharge(key, part):
    key = jax.random.fold_in(key, 11)
    shape = (NZ, NX, NY)
    values = jnp.clip(jax.random.normal(key, shape, jnp.float32), -4.0, 4.0)
    return values


def plant(drawn, rng, least, high):
    longest = drawn.shape.index(max(drawn.shape))
    spots = []
    for shift in (0, 1):
        where = [jax.random.randint(jax.random.fold_in(rng, axis), (), 0, length) for axis, length in enumerate(drawn.shape)]
        where[longest] = (where[longest] + shift) % drawn.shape[longest]
        spots.append(tuple(where))
    return drawn.at[spots[0]].set(least).at[spots[1]].set(high)


def level_of(rng, extent, cuts, low, high):
    def one(position, shards_of):
        draws = jax.random.uniform(jax.random.fold_in(jax.random.fold_in(rng, 6), position), (shards_of,), jnp.float32, low / len(cuts), high / len(cuts))
        return jnp.repeat(jnp.exp(draws), extent[position] // shards_of).reshape((-1,) + (1,) * (len(extent) - position - 1))

    gain = one(*cuts[0])
    for cut in cuts[1:]:
        gain = gain * one(*cut)
    return gain


def gaussian(stream_key, shape, deviation, most, shards=(), held_as=jnp.bfloat16):
    gain = level_of(stream_key, shape, shards, -0.22, 0.18) if shards else 1.0
    entries = jax.random.normal(stream_key, shape, jnp.float32) * deviation * gain
    return jnp.minimum(jnp.maximum(entries, -most), most).astype(held_as)


def setup_inputs(seed: int = 0, part: int = 0) -> dict:
    seeds = jax.random.split(jax.random.key(seed), 7)
    part_splits = jax.random.split(jax.random.fold_in(seeds[6], part), 7)
    return {
        "log_conductivity": gaussian(part_splits[0], (NZ, NX, NY), 0.8, 3.0, ((1, 4),), jnp.float32),
        "storage": jnp.clip(jnp.exp(math.log(0.5) - 2.3025851 * jax.random.uniform(part_splits[1], (NZ, NX, NY), jnp.float32) ** level_of(part_splits[1], (NZ, NX, NY), ((1, 4),), -0.2, 0.2)), 0.05, 0.5),
        "recharge": draw_recharge(jax.random.fold_in(jax.random.fold_in(seeds[6], part), 71), part),
        "pump_cells": plant(jax.random.randint(part_splits[3], (TESTS,), 0, NX * NY * NZ), jax.random.fold_in(part_splits[3], 1), 0, (NX * NY * NZ) - 1).astype(jnp.int32),
        "obs_cells": plant(jax.random.randint(part_splits[4], (TESTS, OBS), 0, NX * NY * NZ), jax.random.fold_in(part_splits[4], 1), 0, (NX * NY * NZ) - 1).astype(jnp.int32),
        "obs_heads": gaussian(part_splits[5], (TESTS, OBS), 0.5, 4.0, ((0, 4),), jnp.float32),
    }


LOW = 0.1
HIGH = 2.0
PUMP_RATE = 8.0
NOISE_VAR = 0.01
NUGGET = 1.0
SMOOTH = 2.0


def conductances(conduct):
    padded = jnp.pad(conduct, 1)
    face_z = 0.5 * (padded[:-1, 1:-1, 1:-1] + padded[1:, 1:-1, 1:-1])
    face_x = 0.5 * (padded[1:-1, :-1, 1:-1] + padded[1:-1, 1:, 1:-1])
    face_y = 0.5 * (padded[1:-1, 1:-1, :-1] + padded[1:-1, 1:-1, 1:])
    return face_z, face_x, face_y


def diagonal_of(face_set, storage):
    face_z, face_x, face_y = face_set
    return storage + face_z[:-1] + face_z[1:] + face_x[:, :-1] + face_x[:, 1:] + face_y[:, :, :-1] + face_y[:, :, 1:]


def operate(values, face_set, storage):
    face_z, face_x, face_y = face_set
    padded = jnp.pad(values, 1)
    result = storage * values
    result = result + face_z[:-1] * (values - padded[:-2, 1:-1, 1:-1]) + face_z[1:] * (values - padded[2:, 1:-1, 1:-1])
    result = result + face_x[:, :-1] * (values - padded[1:-1, :-2, 1:-1]) + face_x[:, 1:] * (values - padded[1:-1, 2:, 1:-1])
    result = result + face_y[:, :, :-1] * (values - padded[1:-1, 1:-1, :-2]) + face_y[:, :, 1:] * (values - padded[1:-1, 1:-1, 2:])
    return result


def chebyshev(rhs_field, apply_op, inverse_diag):
    centre_eig = 0.5 * (HIGH + LOW)
    half_span = 0.5 * (HIGH - LOW)
    ratio_eig = centre_eig / half_span
    rho_old = 1.0 / ratio_eig
    keep_list = []
    step_list = []
    for count_index in range(ITERS):
        rho_new = 1.0 / (2.0 * ratio_eig - rho_old)
        keep_list.append(rho_new * rho_old)
        step_list.append(2.0 * rho_new / half_span)
        rho_old = rho_new
    keep_table = jnp.array(keep_list, jnp.float32)
    step_table = jnp.array(step_list, jnp.float32)
    direction = inverse_diag * rhs_field / centre_eig

    def sweep_body(sweep_index, carry):
        residual, direction, iterate = carry
        residual = residual - apply_op(direction)
        direction = keep_table[sweep_index] * direction + step_table[sweep_index] * (inverse_diag * residual)
        iterate = iterate + direction
        return residual, direction, iterate

    final = lax.fori_loop(0, ITERS, sweep_body, (rhs_field, direction, direction))
    return final[2]


def face_products(head_field, adjoint):
    head_pad = jnp.pad(head_field, 1)
    adj_pad = jnp.pad(adjoint, 1)
    result = (adjoint - adj_pad[:-2, 1:-1, 1:-1]) * (head_field - head_pad[:-2, 1:-1, 1:-1])
    result = result + (adjoint - adj_pad[2:, 1:-1, 1:-1]) * (head_field - head_pad[2:, 1:-1, 1:-1])
    result = result + (adjoint - adj_pad[1:-1, :-2, 1:-1]) * (head_field - head_pad[1:-1, :-2, 1:-1])
    result = result + (adjoint - adj_pad[1:-1, 2:, 1:-1]) * (head_field - head_pad[1:-1, 2:, 1:-1])
    result = result + (adjoint - adj_pad[1:-1, 1:-1, :-2]) * (head_field - head_pad[1:-1, 1:-1, :-2])
    result = result + (adjoint - adj_pad[1:-1, 1:-1, 2:]) * (head_field - head_pad[1:-1, 1:-1, 2:])
    return result


def prior_weight(freq_x_index, full_x, freq_y_index, full_y):
    wave_x = ((freq_x_index + full_x // 2) % full_x - full_x // 2).astype(jnp.float32) * (2.0 * math.pi / full_x)
    wave_y = ((freq_y_index + full_y // 2) % full_y - full_y // 2).astype(jnp.float32) * (2.0 * math.pi / full_y)
    wave_sq = wave_x[:, None] ** 2 + wave_y[None, :] ** 2
    return NUGGET + SMOOTH * CORR ** 2 / (1.0 + CORR ** 2 * wave_sq) ** 2


def reference(log_conductivity, storage, recharge, pump_cells, obs_cells, obs_heads):
    conduct = jnp.exp(log_conductivity)
    face_set = conductances(conduct)
    inverse_diag = 1.0 / diagonal_of(face_set, storage)

    def apply_op(values):
        return operate(values, face_set, storage)

    def one_test(running, inputs):
        pump_cell, obs_cell, obs_value = inputs
        source = recharge.reshape(-1).at[pump_cell].add(-PUMP_RATE).reshape(recharge.shape)
        head_field = chebyshev(source, apply_op, inverse_diag)
        observed = head_field.reshape(-1)[obs_cell]
        misfit = (observed - obs_value) / NOISE_VAR
        adjoint_src = jnp.zeros_like(recharge).reshape(-1).at[obs_cell].add(misfit).reshape(recharge.shape)
        adjoint = chebyshev(adjoint_src, apply_op, inverse_diag)
        return running + face_products(head_field, adjoint), None

    running = lax.scan(one_test, jnp.zeros_like(log_conductivity), (pump_cells, obs_cells, obs_heads))[0]
    gradient = -0.5 * conduct * running
    weights = prior_weight(jnp.arange(NX, dtype=jnp.int32), NX, jnp.arange(NY, dtype=jnp.int32), NY)
    transformed = jnp.fft.fft2(gradient, axes=(1, 2))
    step_field = jnp.real(jnp.fft.ifft2(transformed * weights, axes=(1, 2))).astype(jnp.float32)
    return gradient, step_field
```

```python
import functools
import math

import jax
import jax.numpy as jnp
import numpy as np
from jax import lax
from jax.experimental import pallas as pl
from jax.experimental.pallas import tpu as pltpu
from jax.sharding import PartitionSpec as P

ITERS = 32
CORR = 16
LOW = 0.1
HIGH = 2.0
PUMP_RATE = 8.0
NOISE_VAR = 0.01
NUGGET = 1.0
SMOOTH = 2.0
HIGHEST = lax.Precision.HIGHEST
UNROLL = 8


def sweep_constants():
    centre = 0.5 * (HIGH + LOW)
    span = 0.5 * (HIGH - LOW)
    ratio = centre / span
    rho = 1.0 / ratio
    own, keep, step = [], [], []
    for _ in range(ITERS):
        rho_new = 1.0 / (2.0 * ratio - rho)
        keep.append(rho_new * rho)
        step.append(2.0 * rho_new / span)
        own.append(1.0 + keep[-1] - step[-1])
        rho = rho_new
    return np.array([own, keep, step], np.float32)


def fourier_basis(length):
    where = np.arange(length)
    rows, freqs = [], []
    for freq in range(length // 2 + 1):
        angle = 2.0 * np.pi / length * ((freq * where) % length)
        edge = freq == 0 or 2 * freq == length
        scale = math.sqrt((1.0 if edge else 2.0) / length)
        rows.append(scale * np.cos(angle))
        freqs.append(freq)
        if not edge:
            rows.append(scale * np.sin(angle))
            freqs.append(freq)
    return np.stack(rows), np.array(freqs, np.float64)


def prior_table(freq_x, full_x, freq_y, full_y):
    wave_x = freq_x * (2.0 * np.pi / full_x)
    wave_y = freq_y * (2.0 * np.pi / full_y)
    wave_sq = wave_x[:, None] ** 2 + wave_y[None, :] ** 2
    return NUGGET + SMOOTH * CORR**2 / (1.0 + CORR**2 * wave_sq) ** 2


def solve_kernel(
    slab, consts, place, pump, ports, heads, cells, out,
    cond, inv, c_zm, c_zp, c_xm, c_xp, c_ym, c_yp, rhs, head_a, head_b, adj_a, adj_b,
):
    full_x = cells.shape[0]
    depth, width = cells.shape[2:]
    z_at = lax.broadcasted_iota(jnp.int32, (depth, width), 0)
    y_at = lax.broadcasted_iota(jnp.int32, (depth, width), 1)
    z_lo, z_hi = z_at == 0, z_at == depth - 1
    y_lo, y_hi = y_at == 0, y_at == width - 1
    blank = jnp.zeros((depth, width), jnp.float32)

    def z_before(v):
        return pltpu.roll(v, 1, 0)

    def z_after(v):
        return pltpu.roll(v, depth - 1, 0)

    def y_before(v):
        return pltpu.roll(v, 1, 1)

    def y_after(v):
        return pltpu.roll(v, width - 1, 1)

    for field in (cond, head_a, head_b, adj_a, adj_b):
        field[0] = blank
        field[full_x + 1] = blank

    def rows(body):
        @pl.loop(0, full_x // UNROLL)
        def _(block):
            for inner in range(UNROLL):
                body(block * UNROLL + inner)

    def fill(x):
        cond[x + 1] = jnp.exp(cells[x, 0])

    rows(fill)
    first = 1.0 / (0.5 * (HIGH + LOW))

    def faces(x):
        here = cond[x + 1]
        f_zm = 0.5 * (here + jnp.where(z_lo, 0.0, z_before(here)))
        f_zp = 0.5 * (here + jnp.where(z_hi, 0.0, z_after(here)))
        f_xm = 0.5 * (here + cond[x])
        f_xp = 0.5 * (here + cond[x + 2])
        f_ym = 0.5 * (here + jnp.where(y_lo, 0.0, y_before(here)))
        f_yp = 0.5 * (here + jnp.where(y_hi, 0.0, y_after(here)))
        scale = 1.0 / (cells[x, 1] + f_zm + f_zp + f_xm + f_xp + f_ym + f_yp)
        inv[x] = scale
        c_zm[x] = jnp.where(z_lo, 0.0, f_zm * scale)
        c_zp[x] = jnp.where(z_hi, 0.0, f_zp * scale)
        c_xm[x] = f_xm * scale
        c_xp[x] = f_xp * scale
        c_ym[x] = jnp.where(y_lo, 0.0, f_ym * scale)
        c_yp[x] = jnp.where(y_hi, 0.0, f_yp * scale)
        rhs[x] = cells[x, 2] * scale

    rows(faces)

    def split(cell):
        plane = full_x * width
        rest = lax.rem(cell, plane)
        return lax.div(cell, plane), lax.div(rest, width), lax.rem(rest, width)

    def solve(now, other):
        def start(x):
            now[x + 1] = rhs[x] * first
            other[x + 1] = blank

        rows(start)

        def sweep(src, dst, own, keep, step):
            @pl.loop(0, full_x // UNROLL)
            def _(block):
                base = block * UNROLL
                left = src[base]
                here = src[base + 1]
                for inner in range(UNROLL):
                    x = base + inner
                    right = src[x + 2]
                    total = rhs[x] + c_xm[x] * left + c_xp[x] * right
                    total += c_zm[x] * z_before(here) + c_zp[x] * z_after(here)
                    total += c_ym[x] * y_before(here) + c_yp[x] * y_after(here)
                    dst[x + 1] = own * here - keep * dst[x + 1] + step * total
                    left, here = here, right

        @pl.loop(0, ITERS // 2)
        def _(pair):
            k = 2 * pair
            sweep(now, other, consts[0, k], consts[1, k], consts[2, k])
            sweep(other, now, consts[0, k + 1], consts[1, k + 1], consts[2, k + 1])

    z, x, y = split(pump[0])
    spot = (z_at == z) & (y_at == y)
    rhs[x] = rhs[x] + jnp.where(spot, -PUMP_RATE * inv[x], 0.0)
    solve(head_a, head_b)

    def clear(x):
        rhs[x] = blank

    rows(clear)

    @pl.loop(0, ports.shape[1])
    def _(port):
        z, x, y = split(ports[0, port])
        spot = (z_at == z) & (y_at == y)
        misfit = (head_a[x + 1] - heads[0, port]) * (1.0 / NOISE_VAR)
        rhs[x] = rhs[x] + jnp.where(spot, misfit * inv[x], 0.0)

    solve(adj_a, adj_b)

    first_row = place[0]
    for row in range(slab):
        x = first_row + row
        h, a = head_a[x + 1], adj_a[x + 1]
        total = (a - adj_a[x]) * (h - head_a[x])
        total += (a - adj_a[x + 2]) * (h - head_a[x + 2])
        for move, mask in ((z_before, z_lo), (z_after, z_hi), (y_before, y_lo), (y_after, y_hi)):
            total += (a - jnp.where(mask, 0.0, move(a))) * (h - jnp.where(mask, 0.0, move(h)))
        out[row] = -0.5 * cond[x + 1] * total


def shards(log_conductivity, storage, recharge, pump_cells, obs_cells, obs_heads):
    depth, slab, width = log_conductivity.shape
    dom_count = lax.axis_size("dom")
    dom_index = lax.axis_index("dom")
    full_x = slab * dom_count
    fields = jnp.stack([log_conductivity, storage, recharge]).transpose(2, 0, 1, 3)
    cells = lax.all_gather(fields, "dom", axis=0, tiled=True)
    whole = pltpu.VMEM((full_x, depth, width), jnp.float32)
    padded = pltpu.VMEM((full_x + 2, depth, width), jnp.float32)
    smem = pl.BlockSpec(memory_space=pltpu.SMEM)
    vmem = pl.BlockSpec(memory_space=pltpu.VMEM)
    partial = pl.pallas_call(
        functools.partial(solve_kernel, slab),
        out_shape=jax.ShapeDtypeStruct((slab, depth, width), jnp.float32),
        in_specs=[smem] * 5 + [vmem],
        out_specs=vmem,
        scratch_shapes=[padded] + [whole] * 8 + [padded] * 4,
        compiler_params=pltpu.CompilerParams(vmem_limit_bytes=56 * 1024 * 1024),
    )(
        jnp.asarray(sweep_constants()),
        (dom_index * slab).astype(jnp.int32).reshape(1),
        pump_cells,
        obs_cells,
        obs_heads,
        cells,
    )
    gradient = lax.psum_scatter(
        partial.transpose(1, 0, 2), "test", scatter_dimension=0, tiled=True
    )
    layers = gradient.shape[0]
    basis_x, freq_x = fourier_basis(full_x)
    basis_y, freq_y = fourier_basis(width)
    weights = jnp.asarray(prior_table(freq_x, full_x, freq_y, width), jnp.float32)
    basis_x = jnp.asarray(basis_x, jnp.float32)
    basis_y = jnp.asarray(basis_y, jnp.float32)
    spectral = jnp.dot(gradient.reshape(-1, width), basis_y.T, precision=HIGHEST)
    spectral = lax.all_gather(
        spectral.reshape(layers, slab, width), "dom", axis=1, tiled=True
    )
    filtered = jnp.einsum("fx,mxk->mfk", basis_x, spectral, precision=HIGHEST) * weights
    own_x = lax.dynamic_slice_in_dim(basis_x, dom_index * slab, slab, axis=1)
    back = jnp.einsum("fx,mfk->mxk", own_x, filtered, precision=HIGHEST)
    step_field = jnp.dot(back.reshape(-1, width), basis_y, precision=HIGHEST)
    return gradient, step_field.reshape(layers, slab, width)


def solution(mesh):
    in_specs = (
        P("grp", "dom", None),
        P("grp", "dom", None),
        P("grp", "dom", None),
        P(("grp", "test")),
        P(("grp", "test"), None),
        P(("grp", "test"), None),
    )
    out_specs = (P(("grp", "test"), "dom", None), P(("grp", "test"), "dom", None))
    return jax.shard_map(shards, mesh=mesh, in_specs=in_specs, out_specs=out_specs, check_vma=False)
```

```python
import functools
import math

import jax
import jax.numpy as jnp
import numpy as np
from jax import lax
from jax.experimental import pallas as pl
from jax.experimental.pallas import tpu as pltpu
from jax.sharding import PartitionSpec as P

ITERS = 32
CORR = 16
LOW = 0.1
HIGH = 2.0
PUMP_RATE = 8.0
NOISE_VAR = 0.01
NUGGET = 1.0
SMOOTH = 2.0
HIGHEST = lax.Precision.HIGHEST
UNROLL = 8
MESH = pl.DeviceIdType.MESH
VMEM_LIMIT = 56 * 1024 * 1024


def sweep_constants():
    centre = 0.5 * (HIGH + LOW)
    span = 0.5 * (HIGH - LOW)
    ratio = centre / span
    rho = 1.0 / ratio
    own, keep, step = [], [], []
    for _ in range(ITERS):
        rho_new = 1.0 / (2.0 * ratio - rho)
        keep.append(rho_new * rho)
        step.append(2.0 * rho_new / span)
        own.append(1.0 + keep[-1] - step[-1])
        rho = rho_new
    return np.array([own, keep, step], np.float32)


def fourier_basis(length):
    where = np.arange(length)
    rows, freqs = [], []
    for freq in range(length // 2 + 1):
        angle = 2.0 * np.pi / length * ((freq * where) % length)
        edge = freq == 0 or 2 * freq == length
        scale = math.sqrt((1.0 if edge else 2.0) / length)
        rows.append(scale * np.cos(angle))
        freqs.append(freq)
        if not edge:
            rows.append(scale * np.sin(angle))
            freqs.append(freq)
    return np.stack(rows), np.array(freqs, np.float64)


def prior_table(freq_x, full_x, freq_y, full_y):
    wave_x = freq_x * (2.0 * np.pi / full_x)
    wave_y = freq_y * (2.0 * np.pi / full_y)
    wave_sq = wave_x[:, None] ** 2 + wave_y[None, :] ** 2
    return NUGGET + SMOOTH * CORR**2 / (1.0 + CORR**2 * wave_sq) ** 2


def gather_kernel(
    count, conduct, storage, recharge, cells, near_send, near_recv, far_send, far_recv
):
    slab = conduct.shape[1]
    chips = count // 2
    me = lax.axis_index("dom")
    core, chip = lax.rem(me, 2), lax.div(me, 2)
    twin = me + 1 - 2 * core
    barrier = pltpu.get_barrier_semaphore()

    def far(hop):
        return 2 * lax.rem(chip + hop, chips) + core

    for peer in [twin] + [far(hop) for hop in range(1, chips)]:
        pl.semaphore_signal(barrier, 1, device_id={"dom": peer}, device_id_type=MESH)

    def block(field, owner):
        return cells.at[field, pl.ds(owner * slab, slab)]

    def near_copy(slot, field, owner):
        return pltpu.make_async_remote_copy(
            src_ref=block(field, owner),
            dst_ref=block(field, owner),
            send_sem=near_send.at[slot, field],
            recv_sem=near_recv.at[slot, field],
            device_id={"dom": twin},
            device_id_type=MESH,
        )

    def far_copy(hop, field, owner):
        return pltpu.make_async_remote_copy(
            src_ref=block(field, owner),
            dst_ref=block(field, owner),
            send_sem=far_send.at[hop - 1, field],
            recv_sem=far_recv.at[hop - 1, field],
            device_id={"dom": far(hop)},
            device_id_type=MESH,
        )

    own = pl.ds(me * slab, slab)
    for field, ref in enumerate((conduct, storage, recharge)):
        values = jnp.swapaxes(ref[...], 0, 1)
        cells[field, own] = jnp.exp(values) if field == 0 else values
        if field == 0:
            pl.semaphore_wait(barrier, chips)
        for hop in range(1, chips):
            far_copy(hop, field, me).start()
        near_copy(0, field, me).start()
    for hop in range(1, chips):
        source = far(chips - hop)
        for field in range(3):
            far_copy(hop, field, source).wait_recv()
            near_copy(hop, field, source).start()
    for field in range(3):
        for hop in range(1, chips):
            far_copy(hop, field, me).wait_send()
        for hop in range(chips):
            mine = me if hop == 0 else far(chips - hop)
            near_copy(hop, field, mine).wait_send()
            near_copy(hop, field, mine + 1 - 2 * core).wait_recv()


def reduce_kernel(
    tests, count, part, grad, full, landing, test_send, test_recv, dom_send, dom_recv
):
    layers, slab = grad.shape[:2]
    test, me = lax.axis_index("test"), lax.axis_index("dom")
    barrier = pltpu.get_barrier_semaphore()

    def test_at(hop):
        return lax.rem(test + hop, tests)

    def dom_at(hop):
        return lax.rem(me + hop, count)

    for hop in range(1, tests):
        pl.semaphore_signal(barrier, 1, device_id={"test": test_at(hop)}, device_id_type=MESH)
    for hop in range(1, count):
        pl.semaphore_signal(barrier, 1, device_id={"dom": dom_at(hop)}, device_id_type=MESH)
    pl.semaphore_wait(barrier, tests + count - 2)

    def test_copy(hop):
        return pltpu.make_async_remote_copy(
            src_ref=part.at[pl.ds(test_at(hop) * layers, layers)],
            dst_ref=landing.at[hop - 1],
            send_sem=test_send.at[hop - 1],
            recv_sem=test_recv.at[hop - 1],
            device_id={"test": test_at(hop)},
            device_id_type=MESH,
        )

    def dom_copy(hop, owner):
        place = full.at[:, pl.ds(owner * slab, slab)]
        return pltpu.make_async_remote_copy(
            src_ref=place,
            dst_ref=place,
            send_sem=dom_send.at[hop - 1],
            recv_sem=dom_recv.at[hop - 1],
            device_id={"dom": dom_at(hop)},
            device_id_type=MESH,
        )

    for hop in range(1, tests):
        test_copy(hop).start()
    total = part[pl.ds(test * layers, layers)]
    for hop in range(1, tests):
        test_copy(hop).wait_recv()
        total = total + landing[hop - 1]
    grad[...] = total
    full[:, pl.ds(me * slab, slab)] = total
    for hop in range(1, count):
        dom_copy(hop, me).start()
    for hop in range(1, tests):
        test_copy(hop).wait_send()
    for hop in range(1, count):
        dom_copy(hop, me).wait_send()
        dom_copy(hop, dom_at(count - hop)).wait_recv()


def solve_kernel(
    slab, consts, place, pump, ports, heads, cells, out,
    cond, inv, c_zm, c_zp, c_xm, c_xp, c_ym, c_yp, rhs, head_a, head_b, adj_a, adj_b, terms,
):
    full_x = cells.shape[1]
    depth, width = cells.shape[2:]
    z_at = lax.broadcasted_iota(jnp.int32, (depth, width), 0)
    y_at = lax.broadcasted_iota(jnp.int32, (depth, width), 1)
    z_lo, z_hi = z_at == 0, z_at == depth - 1
    y_lo, y_hi = y_at == 0, y_at == width - 1
    blank = jnp.zeros((depth, width), jnp.float32)

    def z_before(v):
        return pltpu.roll(v, 1, 0)

    def z_after(v):
        return pltpu.roll(v, depth - 1, 0)

    def y_before(v):
        return pltpu.roll(v, 1, 1)

    def y_after(v):
        return pltpu.roll(v, width - 1, 1)

    for field in (cond, head_a, head_b, adj_a, adj_b):
        field[0] = blank
        field[full_x + 1] = blank

    def rows(body):
        @pl.loop(0, full_x // UNROLL)
        def _(block):
            for inner in range(UNROLL):
                body(block * UNROLL + inner)

    def fill(x):
        cond[x + 1] = cells[0, x]

    rows(fill)
    first = 1.0 / (0.5 * (HIGH + LOW))

    def faces(x):
        here = cond[x + 1]
        f_zm = 0.5 * (here + jnp.where(z_lo, 0.0, z_before(here)))
        f_zp = 0.5 * (here + jnp.where(z_hi, 0.0, z_after(here)))
        f_xm = 0.5 * (here + cond[x])
        f_xp = 0.5 * (here + cond[x + 2])
        f_ym = 0.5 * (here + jnp.where(y_lo, 0.0, y_before(here)))
        f_yp = 0.5 * (here + jnp.where(y_hi, 0.0, y_after(here)))
        scale = 1.0 / (cells[1, x] + f_zm + f_zp + f_xm + f_xp + f_ym + f_yp)
        inv[x] = scale
        c_zm[x] = jnp.where(z_lo, 0.0, f_zm * scale)
        c_zp[x] = jnp.where(z_hi, 0.0, f_zp * scale)
        c_xm[x] = f_xm * scale
        c_xp[x] = f_xp * scale
        c_ym[x] = jnp.where(y_lo, 0.0, f_ym * scale)
        c_yp[x] = jnp.where(y_hi, 0.0, f_yp * scale)
        rhs[x] = cells[2, x] * scale

    rows(faces)

    def split(cell):
        plane = full_x * width
        rest = lax.rem(cell, plane)
        return lax.div(cell, plane), lax.div(rest, width), lax.rem(rest, width)

    def solve(now, other):
        def start(x):
            now[x + 1] = rhs[x] * first
            other[x + 1] = blank

        rows(start)

        def sweep(src, dst, own, keep, step):
            @pl.loop(0, full_x // UNROLL)
            def _(block):
                base = block * UNROLL
                left = src[base]
                here = src[base + 1]
                for inner in range(UNROLL):
                    x = base + inner
                    right = src[x + 2]
                    total = rhs[x] + c_xm[x] * left + c_xp[x] * right
                    total += c_zm[x] * z_before(here) + c_zp[x] * z_after(here)
                    total += c_ym[x] * y_before(here) + c_yp[x] * y_after(here)
                    dst[x + 1] = own * here - keep * dst[x + 1] + step * total
                    left, here = here, right

        @pl.loop(0, ITERS // 2)
        def _(pair):
            k = 2 * pair
            sweep(now, other, consts[0, k], consts[1, k], consts[2, k])
            sweep(other, now, consts[0, k + 1], consts[1, k + 1], consts[2, k + 1])

    z, x, y = split(pump[0])
    spot = (z_at == z) & (y_at == y)
    rhs[x] = rhs[x] + jnp.where(spot, -PUMP_RATE * inv[x], 0.0)
    solve(head_a, head_b)

    def clear(x):
        rhs[x] = blank

    rows(clear)

    @pl.loop(0, ports.shape[1])
    def _(port):
        z, x, y = split(ports[0, port])
        spot = (z_at == z) & (y_at == y)
        misfit = (head_a[x + 1] - heads[0, port]) * (1.0 / NOISE_VAR)
        rhs[x] = rhs[x] + jnp.where(spot, misfit * inv[x], 0.0)

    solve(adj_a, adj_b)

    first_row = place[0]
    for row in range(slab):
        x = first_row + row
        h, a = head_a[x + 1], adj_a[x + 1]
        total = (a - adj_a[x]) * (h - head_a[x])
        total += (a - adj_a[x + 2]) * (h - head_a[x + 2])
        for move, mask in ((z_before, z_lo), (z_after, z_hi), (y_before, y_lo), (y_after, y_hi)):
            total += (a - jnp.where(mask, 0.0, move(a))) * (h - jnp.where(mask, 0.0, move(h)))
        terms[row] = -0.5 * cond[x + 1] * total
    out[...] = jnp.swapaxes(terms[...], 0, 1)


def shards(log_conductivity, storage, recharge, pump_cells, obs_cells, obs_heads):
    depth, slab, width = log_conductivity.shape
    dom_count = lax.axis_size("dom")
    dom_index = lax.axis_index("dom")
    full_x = slab * dom_count
    whole = pltpu.VMEM((full_x, depth, width), jnp.float32)
    padded = pltpu.VMEM((full_x + 2, depth, width), jnp.float32)
    smem = pl.BlockSpec(memory_space=pltpu.SMEM)
    vmem = pl.BlockSpec(memory_space=pltpu.VMEM)
    chips = dom_count // 2
    cells = pl.pallas_call(
        functools.partial(gather_kernel, dom_count),
        out_shape=jax.ShapeDtypeStruct((3, full_x, depth, width), jnp.float32),
        in_specs=[vmem] * 3,
        out_specs=vmem,
        scratch_shapes=[pltpu.SemaphoreType.DMA((chips, 3))] * 2
        + [pltpu.SemaphoreType.DMA((max(chips - 1, 1), 3))] * 2,
        compiler_params=pltpu.CompilerParams(
            collective_id=0, has_side_effects=True, vmem_limit_bytes=VMEM_LIMIT
        ),
    )(log_conductivity, storage, recharge)
    partial = pl.pallas_call(
        functools.partial(solve_kernel, slab),
        out_shape=jax.ShapeDtypeStruct((depth, slab, width), jnp.float32),
        in_specs=[smem] * 5 + [vmem],
        out_specs=vmem,
        scratch_shapes=[padded] + [whole] * 8 + [padded] * 4
        + [pltpu.VMEM((slab, depth, width), jnp.float32)],
        compiler_params=pltpu.CompilerParams(vmem_limit_bytes=VMEM_LIMIT),
    )(
        jnp.asarray(sweep_constants()),
        (dom_index * slab).astype(jnp.int32).reshape(1),
        pump_cells,
        obs_cells,
        obs_heads,
        cells,
    )
    tests = lax.axis_size("test")
    layers = depth // tests
    gradient, full = pl.pallas_call(
        functools.partial(reduce_kernel, tests, dom_count),
        out_shape=(
            jax.ShapeDtypeStruct((layers, slab, width), jnp.float32),
            jax.ShapeDtypeStruct((layers, full_x, width), jnp.float32),
        ),
        in_specs=[vmem],
        out_specs=(vmem, vmem),
        scratch_shapes=[pltpu.VMEM((tests - 1, layers, slab, width), jnp.float32)]
        + [pltpu.SemaphoreType.DMA((tests - 1,))] * 2
        + [pltpu.SemaphoreType.DMA((dom_count - 1,))] * 2,
        compiler_params=pltpu.CompilerParams(
            collective_id=1, has_side_effects=True, vmem_limit_bytes=VMEM_LIMIT
        ),
    )(partial)
    basis_x, freq_x = fourier_basis(full_x)
    basis_y, freq_y = fourier_basis(width)
    weights = jnp.asarray(prior_table(freq_x, full_x, freq_y, width), jnp.float32)
    basis_x = jnp.asarray(basis_x, jnp.float32)
    basis_y = jnp.asarray(basis_y, jnp.float32)
    spectral = jnp.dot(full.reshape(-1, width), basis_y.T, precision=HIGHEST)
    spectral = spectral.reshape(layers, full_x, width)
    filtered = jnp.einsum("fx,mxk->mfk", basis_x, spectral, precision=HIGHEST) * weights
    own_x = lax.dynamic_slice_in_dim(basis_x, dom_index * slab, slab, axis=1)
    back = jnp.einsum("fx,mfk->mxk", own_x, filtered, precision=HIGHEST)
    step_field = jnp.dot(back.reshape(-1, width), basis_y, precision=HIGHEST)
    return gradient, step_field.reshape(layers, slab, width)


def solution(mesh):
    in_specs = (
        P("grp", "dom", None),
        P("grp", "dom", None),
        P("grp", "dom", None),
        P(("grp", "test")),
        P(("grp", "test"), None),
        P(("grp", "test"), None),
    )
    out_specs = (P(("grp", "test"), "dom", None), P(("grp", "test"), "dom", None))
    return jax.shard_map(shards, mesh=mesh, in_specs=in_specs, out_specs=out_specs, check_vma=False)
```

```python
import functools
import math

import jax
import jax.numpy as jnp
import numpy as np
from jax import lax
from jax.experimental import pallas as pl
from jax.experimental.pallas import tpu as pltpu
from jax.sharding import PartitionSpec as P

ITERS = 32
CORR = 16
LOW = 0.1
HIGH = 2.0
PUMP_RATE = 8.0
NOISE_VAR = 0.01
NUGGET = 1.0
SMOOTH = 2.0
HIGHEST = lax.Precision.HIGHEST
SUBLANES = 8
LANES = 128
MESH = pl.DeviceIdType.MESH
VMEM_LIMIT = 56 * 1024 * 1024


def sweep_constants():
    centre = 0.5 * (HIGH + LOW)
    span = 0.5 * (HIGH - LOW)
    ratio = centre / span
    rho = 1.0 / ratio
    own, keep, step = [], [], []
    for _ in range(ITERS):
        rho_new = 1.0 / (2.0 * ratio - rho)
        keep.append(rho_new * rho)
        step.append(2.0 * rho_new / span)
        own.append(1.0 + keep[-1] - step[-1])
        rho = rho_new
    return np.array([own, keep, step], np.float32)


def fourier_basis(length):
    where = np.arange(length)
    rows, freqs = [], []
    for freq in range(length // 2 + 1):
        angle = 2.0 * np.pi / length * ((freq * where) % length)
        edge = freq == 0 or 2 * freq == length
        scale = math.sqrt((1.0 if edge else 2.0) / length)
        rows.append(scale * np.cos(angle))
        freqs.append(freq)
        if not edge:
            rows.append(scale * np.sin(angle))
            freqs.append(freq)
    return np.stack(rows), np.array(freqs, np.float64)


def prior_table(freq_x, full_x, freq_y, full_y):
    wave_x = freq_x * (2.0 * np.pi / full_x)
    wave_y = freq_y * (2.0 * np.pi / full_y)
    wave_sq = wave_x[:, None] ** 2 + wave_y[None, :] ** 2
    return NUGGET + SMOOTH * CORR**2 / (1.0 + CORR**2 * wave_sq) ** 2


def gather_kernel(
    count, conduct, storage, recharge, cells, near_send, near_recv, far_send, far_recv
):
    slab = conduct.shape[1]
    chips = count // 2
    me = lax.axis_index("dom")
    core, chip = lax.rem(me, 2), lax.div(me, 2)
    twin = me + 1 - 2 * core
    barrier = pltpu.get_barrier_semaphore()

    def far(hop):
        return 2 * lax.rem(chip + hop, chips) + core

    for peer in [twin] + [far(hop) for hop in range(1, chips)]:
        pl.semaphore_signal(barrier, 1, device_id={"dom": peer}, device_id_type=MESH)

    def block(field, owner):
        return cells.at[field, :, pl.ds(owner * slab, slab)]

    def near_copy(slot, field, owner):
        return pltpu.make_async_remote_copy(
            src_ref=block(field, owner),
            dst_ref=block(field, owner),
            send_sem=near_send.at[slot, field],
            recv_sem=near_recv.at[slot, field],
            device_id={"dom": twin},
            device_id_type=MESH,
        )

    def far_copy(hop, field, owner):
        return pltpu.make_async_remote_copy(
            src_ref=block(field, owner),
            dst_ref=block(field, owner),
            send_sem=far_send.at[hop - 1, field],
            recv_sem=far_recv.at[hop - 1, field],
            device_id={"dom": far(hop)},
            device_id_type=MESH,
        )

    own = pl.ds(me * slab, slab)
    for field, ref in enumerate((conduct, storage, recharge)):
        values = jnp.swapaxes(ref[...], 0, 1)
        values = jnp.exp(values) if field == 0 else values
        for lane in range(cells.shape[1]):
            cells[field, lane, own] = values[:, :, lane * LANES : (lane + 1) * LANES]
        if field == 0:
            pl.semaphore_wait(barrier, chips)
        for hop in range(1, chips):
            far_copy(hop, field, me).start()
        near_copy(0, field, me).start()
    for hop in range(1, chips):
        source = far(chips - hop)
        for field in range(3):
            far_copy(hop, field, source).wait_recv()
            near_copy(hop, field, source).start()
    for field in range(3):
        for hop in range(1, chips):
            far_copy(hop, field, me).wait_send()
        for hop in range(chips):
            mine = me if hop == 0 else far(chips - hop)
            near_copy(hop, field, mine).wait_send()
            near_copy(hop, field, mine + 1 - 2 * core).wait_recv()


def reduce_kernel(
    tests, count, part, grad, full, landing, test_send, test_recv, dom_send, dom_recv
):
    layers, slab = grad.shape[:2]
    test, me = lax.axis_index("test"), lax.axis_index("dom")
    barrier = pltpu.get_barrier_semaphore()

    def test_at(hop):
        return lax.rem(test + hop, tests)

    def dom_at(hop):
        return lax.rem(me + hop, count)

    for hop in range(1, tests):
        pl.semaphore_signal(barrier, 1, device_id={"test": test_at(hop)}, device_id_type=MESH)
    for hop in range(1, count):
        pl.semaphore_signal(barrier, 1, device_id={"dom": dom_at(hop)}, device_id_type=MESH)
    pl.semaphore_wait(barrier, tests + count - 2)

    def test_copy(hop):
        return pltpu.make_async_remote_copy(
            src_ref=part.at[pl.ds(test_at(hop) * layers, layers)],
            dst_ref=landing.at[hop - 1],
            send_sem=test_send.at[hop - 1],
            recv_sem=test_recv.at[hop - 1],
            device_id={"test": test_at(hop)},
            device_id_type=MESH,
        )

    def dom_copy(hop, owner):
        place = full.at[:, pl.ds(owner * slab, slab)]
        return pltpu.make_async_remote_copy(
            src_ref=place,
            dst_ref=place,
            send_sem=dom_send.at[hop - 1],
            recv_sem=dom_recv.at[hop - 1],
            device_id={"dom": dom_at(hop)},
            device_id_type=MESH,
        )

    for hop in range(1, tests):
        test_copy(hop).start()
    total = part[pl.ds(test * layers, layers)]
    for hop in range(1, tests):
        test_copy(hop).wait_recv()
        total = total + landing[hop - 1]
    grad[...] = total
    full[:, pl.ds(me * slab, slab)] = total
    for hop in range(1, count):
        dom_copy(hop, me).start()
    for hop in range(1, tests):
        test_copy(hop).wait_send()
    for hop in range(1, count):
        dom_copy(hop, me).wait_send()
        dom_copy(hop, dom_at(count - hop)).wait_recv()


def solve_kernel(
    slab, consts, place, pump, ports, heads, cells, out,
    cond, inv, c_zm, c_zp, c_xm, c_xp, c_ym, c_yp, rhs, head_a, head_b, adj_a, adj_b, terms,
):
    depth = out.shape[0]
    width = out.shape[2]
    full_x = cells.shape[2] // depth
    tiles = full_x // SUBLANES
    s_at = lax.broadcasted_iota(jnp.int32, (SUBLANES, width), 0)
    y_at = lax.broadcasted_iota(jnp.int32, (SUBLANES, width), 1)
    y_lo, y_hi = y_at == 0, y_at == width - 1
    blank = jnp.zeros((SUBLANES, width), jnp.float32)

    def s_before(v):
        return pltpu.roll(v, 1, 0)

    def s_after(v):
        return pltpu.roll(v, SUBLANES - 1, 0)

    def y_before(v):
        return pltpu.roll(v, 1, 1)

    def y_after(v):
        return pltpu.roll(v, width - 1, 1)

    def rows(body):
        @pl.loop(0, tiles)
        def _(t):
            for z in range(depth):
                body(t, z)

    def wrap(field):
        for z in range(depth):
            field[0, z] = s_before(field[tiles, z])
            field[tiles + 1, z] = s_after(field[1, z])

    def ends(t):
        x_at = s_at * tiles + t
        return x_at == 0, x_at == full_x - 1

    def strided(field, t, z):
        at = pl.ds(t * depth + z, SUBLANES, stride=tiles * depth)
        return jnp.concatenate(
            [cells[field, lane, at] for lane in range(width // LANES)], axis=1
        )

    def fill(t, z):
        cond[t + 1, z] = strided(0, t, z)

    rows(fill)
    wrap(cond)
    first = 1.0 / (0.5 * (HIGH + LOW))

    def faces(t, z):
        x_lo, x_hi = ends(t)
        here = cond[t + 1, z]
        f_zm = 0.5 * (here + cond[t + 1, z - 1]) if z > 0 else 0.5 * here
        f_zp = 0.5 * (here + cond[t + 1, z + 1]) if z < depth - 1 else 0.5 * here
        f_xm = 0.5 * (here + jnp.where(x_lo, 0.0, cond[t, z]))
        f_xp = 0.5 * (here + jnp.where(x_hi, 0.0, cond[t + 2, z]))
        f_ym = 0.5 * (here + jnp.where(y_lo, 0.0, y_before(here)))
        f_yp = 0.5 * (here + jnp.where(y_hi, 0.0, y_after(here)))
        scale = 1.0 / (strided(1, t, z) + f_zm + f_zp + f_xm + f_xp + f_ym + f_yp)
        inv[t, z] = scale
        c_zm[t, z] = f_zm * scale
        c_zp[t, z] = f_zp * scale
        c_xm[t, z] = jnp.where(x_lo, 0.0, f_xm * scale)
        c_xp[t, z] = jnp.where(x_hi, 0.0, f_xp * scale)
        c_ym[t, z] = jnp.where(y_lo, 0.0, f_ym * scale)
        c_yp[t, z] = jnp.where(y_hi, 0.0, f_yp * scale)
        rhs[t, z] = strided(2, t, z) * scale

    rows(faces)

    def split(cell):
        plane = full_x * width
        rest = lax.rem(cell, plane)
        x, y = lax.div(rest, width), lax.rem(rest, width)
        spot = (s_at == lax.div(x, tiles)) & (y_at == y)
        return lax.div(cell, plane), lax.rem(x, tiles), spot

    def solve(now, other):
        def start(t, z):
            now[t + 1, z] = rhs[t, z] * first
            other[t + 1, z] = blank

        rows(start)
        wrap(now)

        def sweep(src, dst, own, keep, step):
            @pl.loop(0, tiles)
            def _(t):
                here = src[t + 1, 0]
                for z in range(depth):
                    total = rhs[t, z] + c_xm[t, z] * src[t, z] + c_xp[t, z] * src[t + 2, z]
                    total += c_ym[t, z] * y_before(here) + c_yp[t, z] * y_after(here)
                    if z > 0:
                        total += c_zm[t, z] * before
                    if z < depth - 1:
                        after = src[t + 1, z + 1]
                        total += c_zp[t, z] * after
                    dst[t + 1, z] = own * here - keep * dst[t + 1, z] + step * total
                    before, here = here, after

            wrap(dst)

        @pl.loop(0, ITERS // 2)
        def _(pair):
            k = 2 * pair
            sweep(now, other, consts[0, k], consts[1, k], consts[2, k])
            sweep(other, now, consts[0, k + 1], consts[1, k + 1], consts[2, k + 1])

    z, t, spot = split(pump[0])
    rhs[t, z] = rhs[t, z] + jnp.where(spot, -PUMP_RATE * inv[t, z], 0.0)
    solve(head_a, head_b)

    def clear(t, z):
        rhs[t, z] = blank

    rows(clear)

    @pl.loop(0, ports.shape[1])
    def _(port):
        z, t, spot = split(ports[0, port])
        misfit = (head_a[t + 1, z] - heads[0, port]) * (1.0 / NOISE_VAR)
        rhs[t, z] = rhs[t, z] + jnp.where(spot, misfit * inv[t, z], 0.0)

    solve(adj_a, adj_b)

    def products(t, z):
        h, a = head_a[t + 1, z], adj_a[t + 1, z]

        def at(mask, h_near, a_near):
            return (a - jnp.where(mask, 0.0, a_near)) * (h - jnp.where(mask, 0.0, h_near))

        x_lo, x_hi = ends(t)
        total = at(x_lo, head_a[t, z], adj_a[t, z])
        total += at(x_hi, head_a[t + 2, z], adj_a[t + 2, z])
        total += at(y_lo, y_before(h), y_before(a))
        total += at(y_hi, y_after(h), y_after(a))
        for near in (z - 1, z + 1):
            if 0 <= near < depth:
                total += (a - adj_a[t + 1, near]) * (h - head_a[t + 1, near])
            else:
                total += a * h
        total = -0.5 * cond[t + 1, z] * total
        at_rows = pl.ds(z * full_x + t, SUBLANES, stride=tiles)
        for lane in range(width // LANES):
            terms[lane, at_rows] = total[:, lane * LANES : (lane + 1) * LANES]

    rows(products)
    for z in range(depth):
        own = pl.ds(pl.multiple_of(z * full_x + place[0], SUBLANES), slab)
        for lane in range(width // LANES):
            out[z, :, lane * LANES : (lane + 1) * LANES] = terms[lane, own]


def shards(log_conductivity, storage, recharge, pump_cells, obs_cells, obs_heads):
    depth, slab, width = log_conductivity.shape
    dom_count = lax.axis_size("dom")
    dom_index = lax.axis_index("dom")
    full_x = slab * dom_count
    tiles = full_x // SUBLANES
    whole = pltpu.VMEM((tiles, depth, SUBLANES, width), jnp.float32)
    padded = pltpu.VMEM((tiles + 2, depth, SUBLANES, width), jnp.float32)
    smem = pl.BlockSpec(memory_space=pltpu.SMEM)
    vmem = pl.BlockSpec(memory_space=pltpu.VMEM)
    chips = dom_count // 2
    cells = pl.pallas_call(
        functools.partial(gather_kernel, dom_count),
        out_shape=jax.ShapeDtypeStruct((3, width // LANES, full_x, depth, LANES), jnp.float32),
        in_specs=[vmem] * 3,
        out_specs=vmem,
        scratch_shapes=[pltpu.SemaphoreType.DMA((chips, 3))] * 2
        + [pltpu.SemaphoreType.DMA((max(chips - 1, 1), 3))] * 2,
        compiler_params=pltpu.CompilerParams(
            collective_id=0, has_side_effects=True, vmem_limit_bytes=VMEM_LIMIT
        ),
    )(log_conductivity, storage, recharge)
    partial = pl.pallas_call(
        functools.partial(solve_kernel, slab),
        out_shape=jax.ShapeDtypeStruct((depth, slab, width), jnp.float32),
        in_specs=[smem] * 5 + [vmem],
        out_specs=vmem,
        scratch_shapes=[padded] + [whole] * 8 + [padded] * 4
        + [pltpu.VMEM((width // LANES, depth * full_x, LANES), jnp.float32)],
        compiler_params=pltpu.CompilerParams(vmem_limit_bytes=VMEM_LIMIT),
    )(
        jnp.asarray(sweep_constants()),
        (dom_index * slab).astype(jnp.int32).reshape(1),
        pump_cells,
        obs_cells,
        obs_heads,
        cells.reshape(3, width // LANES, full_x * depth, LANES),
    )
    tests = lax.axis_size("test")
    layers = depth // tests
    gradient, full = pl.pallas_call(
        functools.partial(reduce_kernel, tests, dom_count),
        out_shape=(
            jax.ShapeDtypeStruct((layers, slab, width), jnp.float32),
            jax.ShapeDtypeStruct((layers, full_x, width), jnp.float32),
        ),
        in_specs=[vmem],
        out_specs=(vmem, vmem),
        scratch_shapes=[pltpu.VMEM((tests - 1, layers, slab, width), jnp.float32)]
        + [pltpu.SemaphoreType.DMA((tests - 1,))] * 2
        + [pltpu.SemaphoreType.DMA((dom_count - 1,))] * 2,
        compiler_params=pltpu.CompilerParams(
            collective_id=1, has_side_effects=True, vmem_limit_bytes=VMEM_LIMIT
        ),
    )(partial)
    basis_x, freq_x = fourier_basis(full_x)
    basis_y, freq_y = fourier_basis(width)
    weights = jnp.asarray(prior_table(freq_x, full_x, freq_y, width), jnp.float32)
    basis_x = jnp.asarray(basis_x, jnp.float32)
    basis_y = jnp.asarray(basis_y, jnp.float32)
    spectral = jnp.dot(full.reshape(-1, width), basis_y.T, precision=HIGHEST)
    spectral = spectral.reshape(layers, full_x, width)
    filtered = jnp.einsum("fx,mxk->mfk", basis_x, spectral, precision=HIGHEST) * weights
    own_x = lax.dynamic_slice_in_dim(basis_x, dom_index * slab, slab, axis=1)
    back = jnp.einsum("fx,mfk->mxk", own_x, filtered, precision=HIGHEST)
    step_field = jnp.dot(back.reshape(-1, width), basis_y, precision=HIGHEST)
    return gradient, step_field.reshape(layers, slab, width)


def solution(mesh):
    in_specs = (
        P("grp", "dom", None),
        P("grp", "dom", None),
        P("grp", "dom", None),
        P(("grp", "test")),
        P(("grp", "test"), None),
        P(("grp", "test"), None),
    )
    out_specs = (P(("grp", "test"), "dom", None), P(("grp", "test"), "dom", None))
    return jax.shard_map(shards, mesh=mesh, in_specs=in_specs, out_specs=out_specs, check_vma=False)
```

```python
import functools
import math

import jax
import jax.numpy as jnp
import numpy as np
from jax import lax
from jax.experimental import pallas as pl
from jax.experimental.pallas import tpu as pltpu
from jax.sharding import PartitionSpec as P

ITERS = 32
CORR = 16
LOW = 0.1
HIGH = 2.0
PUMP_RATE = 8.0
NOISE_VAR = 0.01
NUGGET = 1.0
SMOOTH = 2.0
HIGHEST = lax.Precision.HIGHEST
UNROLL = 8
MESH = pl.DeviceIdType.MESH
VMEM_LIMIT = 56 * 1024 * 1024


def sweep_constants():
    centre = 0.5 * (HIGH + LOW)
    span = 0.5 * (HIGH - LOW)
    ratio = centre / span
    rho = 1.0 / ratio
    own, keep, step = [], [], []
    for _ in range(ITERS):
        rho_new = 1.0 / (2.0 * ratio - rho)
        keep.append(rho_new * rho)
        step.append(2.0 * rho_new / span)
        own.append(1.0 + keep[-1] - step[-1])
        rho = rho_new
    return np.array([own, keep, step], np.float32)


def fourier_basis(length):
    where = np.arange(length)
    rows, freqs = [], []
    for freq in range(length // 2 + 1):
        angle = 2.0 * np.pi / length * ((freq * where) % length)
        edge = freq == 0 or 2 * freq == length
        scale = math.sqrt((1.0 if edge else 2.0) / length)
        rows.append(scale * np.cos(angle))
        freqs.append(freq)
        if not edge:
            rows.append(scale * np.sin(angle))
            freqs.append(freq)
    return np.stack(rows), np.array(freqs, np.float64)


def prior_table(freq_x, full_x, freq_y, full_y):
    wave_x = freq_x * (2.0 * np.pi / full_x)
    wave_y = freq_y * (2.0 * np.pi / full_y)
    wave_sq = wave_x[:, None] ** 2 + wave_y[None, :] ** 2
    return NUGGET + SMOOTH * CORR**2 / (1.0 + CORR**2 * wave_sq) ** 2


def gather_kernel(
    count, conduct, storage, recharge, cells, near_send, near_recv, far_send, far_recv
):
    slab = conduct.shape[1]
    chips = count // 2
    me = lax.axis_index("dom")
    core, chip = lax.rem(me, 2), lax.div(me, 2)
    twin = me + 1 - 2 * core
    barrier = pltpu.get_barrier_semaphore()

    def far(hop):
        return 2 * lax.rem(chip + hop, chips) + core

    for peer in [twin] + [far(hop) for hop in range(1, chips)]:
        pl.semaphore_signal(barrier, 1, device_id={"dom": peer}, device_id_type=MESH)

    def block(field, owner):
        return cells.at[field, pl.ds(owner * slab, slab)]

    def near_copy(slot, field, owner):
        return pltpu.make_async_remote_copy(
            src_ref=block(field, owner),
            dst_ref=block(field, owner),
            send_sem=near_send.at[slot, field],
            recv_sem=near_recv.at[slot, field],
            device_id={"dom": twin},
            device_id_type=MESH,
        )

    def far_copy(hop, field, owner):
        return pltpu.make_async_remote_copy(
            src_ref=block(field, owner),
            dst_ref=block(field, owner),
            send_sem=far_send.at[hop - 1, field],
            recv_sem=far_recv.at[hop - 1, field],
            device_id={"dom": far(hop)},
            device_id_type=MESH,
        )

    own = pl.ds(me * slab, slab)
    for field, ref in enumerate((conduct, storage, recharge)):
        values = jnp.swapaxes(ref[...], 0, 1)
        cells[field, own] = jnp.exp(values) if field == 0 else values
        if field == 0:
            pl.semaphore_wait(barrier, chips)
        for hop in range(1, chips):
            far_copy(hop, field, me).start()
        near_copy(0, field, me).start()
    for hop in range(1, chips):
        source = far(chips - hop)
        for field in range(3):
            far_copy(hop, field, source).wait_recv()
            near_copy(hop, field, source).start()
    for field in range(3):
        for hop in range(1, chips):
            far_copy(hop, field, me).wait_send()
        for hop in range(chips):
            mine = me if hop == 0 else far(chips - hop)
            near_copy(hop, field, mine).wait_send()
            near_copy(hop, field, mine + 1 - 2 * core).wait_recv()


def reduce_kernel(
    tests, count, part, grad, full, landing, test_send, test_recv, dom_send, dom_recv
):
    layers, slab = grad.shape[:2]
    test, me = lax.axis_index("test"), lax.axis_index("dom")
    barrier = pltpu.get_barrier_semaphore()

    def test_at(hop):
        return lax.rem(test + hop, tests)

    def dom_at(hop):
        return lax.rem(me + hop, count)

    for hop in range(1, tests):
        pl.semaphore_signal(barrier, 1, device_id={"test": test_at(hop)}, device_id_type=MESH)
    for hop in range(1, count):
        pl.semaphore_signal(barrier, 1, device_id={"dom": dom_at(hop)}, device_id_type=MESH)
    pl.semaphore_wait(barrier, tests + count - 2)

    def test_copy(hop):
        return pltpu.make_async_remote_copy(
            src_ref=part.at[pl.ds(test_at(hop) * layers, layers)],
            dst_ref=landing.at[hop - 1],
            send_sem=test_send.at[hop - 1],
            recv_sem=test_recv.at[hop - 1],
            device_id={"test": test_at(hop)},
            device_id_type=MESH,
        )

    def dom_copy(hop, owner):
        place = full.at[:, pl.ds(owner * slab, slab)]
        return pltpu.make_async_remote_copy(
            src_ref=place,
            dst_ref=place,
            send_sem=dom_send.at[hop - 1],
            recv_sem=dom_recv.at[hop - 1],
            device_id={"dom": dom_at(hop)},
            device_id_type=MESH,
        )

    for hop in range(1, tests):
        test_copy(hop).start()
    total = part[pl.ds(test * layers, layers)]
    for hop in range(1, tests):
        test_copy(hop).wait_recv()
        total = total + landing[hop - 1]
    grad[...] = total
    full[:, pl.ds(me * slab, slab)] = total
    for hop in range(1, count):
        dom_copy(hop, me).start()
    for hop in range(1, tests):
        test_copy(hop).wait_send()
    for hop in range(1, count):
        dom_copy(hop, me).wait_send()
        dom_copy(hop, dom_at(count - hop)).wait_recv()


def solve_kernel(
    slab, consts, place, pump, ports, heads, cells, out,
    cond, scale, c_x, c_y, c_z, rhs, head_a, head_b, adj_a, adj_b, terms,
):
    full_x = cells.shape[1]
    depth, width = cells.shape[2:]
    z_at = lax.broadcasted_iota(jnp.int32, (depth, width), 0)
    y_at = lax.broadcasted_iota(jnp.int32, (depth, width), 1)
    z_lo, z_hi = z_at == 0, z_at == depth - 1
    y_lo, y_hi = y_at == 0, y_at == width - 1
    blank = jnp.zeros((depth, width), jnp.float32)

    def z_before(v):
        return pltpu.roll(v, 1, 0)

    def z_after(v):
        return pltpu.roll(v, depth - 1, 0)

    def y_before(v):
        return pltpu.roll(v, 1, 1)

    def y_after(v):
        return pltpu.roll(v, width - 1, 1)

    for field in (cond, scale, c_x, head_a, head_b, adj_a, adj_b):
        field[0] = blank
        field[full_x + 1] = blank

    def rows(body):
        @pl.loop(0, full_x // UNROLL)
        def _(block):
            for inner in range(UNROLL):
                body(block * UNROLL + inner)

    def fill(x):
        cond[x + 1] = cells[0, x]

    c_x[full_x] = blank
    rows(fill)
    first = 1.0 / (0.5 * (HIGH + LOW))

    def faces(x):
        here = cond[x + 1]
        f_zm = 0.5 * (here + jnp.where(z_lo, 0.0, z_before(here)))
        f_zp = 0.5 * (here + jnp.where(z_hi, 0.0, z_after(here)))
        f_xm = 0.5 * (here + cond[x])
        f_xp = 0.5 * (here + cond[x + 2])
        f_ym = 0.5 * (here + jnp.where(y_lo, 0.0, y_before(here)))
        f_yp = 0.5 * (here + jnp.where(y_hi, 0.0, y_after(here)))
        root = 1.0 / jnp.sqrt(cells[1, x] + f_zm + f_zp + f_xm + f_xp + f_ym + f_yp)
        scale[x + 1] = root
        c_x[x] = f_xm
        c_y[x] = f_yp
        c_z[x] = f_zp
        rhs[x] = cells[2, x] * root

    rows(faces)

    def couple(x):
        root = scale[x + 1]
        c_x[x] = c_x[x] * root * scale[x]
        c_y[x] = jnp.where(y_hi, 0.0, c_y[x] * root * y_after(root))
        c_z[x] = jnp.where(z_hi, 0.0, c_z[x] * root * z_after(root))

    rows(couple)

    def split(cell):
        plane = full_x * width
        rest = lax.rem(cell, plane)
        return lax.div(cell, plane), lax.div(rest, width), lax.rem(rest, width)

    def solve(now, other, near_slab):
        def start(x):
            now[x + 1] = rhs[x] * first
            other[x + 1] = blank

        rows(start)

        def sweep(src, dst, k):
            own, keep, step = consts[0, k], consts[1, k], consts[2, k]
            low, high = 0, full_x // UNROLL
            if near_slab:
                reach = ITERS - k
                low = lax.div(jnp.maximum(place[0] - reach, 0), UNROLL)
                high = lax.div(jnp.minimum(place[0] + slab + reach, full_x) + UNROLL - 1, UNROLL)

            @pl.loop(low, high)
            def _(block):
                base = block * UNROLL
                left = c_x[base] * src[base]
                here = src[base + 1]
                for inner in range(UNROLL):
                    x = base + inner
                    right = src[x + 2]
                    face_x, face_y, face_z = c_x[x + 1], c_y[x], c_z[x]
                    total = rhs[x] + left + face_x * right
                    total += face_z * z_after(here) + z_before(face_z * here)
                    total += face_y * y_after(here) + y_before(face_y * here)
                    dst[x + 1] = own * here - keep * dst[x + 1] + step * total
                    left, here = face_x * here, right

        @pl.loop(0, ITERS // 2)
        def _(pair):
            sweep(now, other, 2 * pair)
            sweep(other, now, 2 * pair + 1)

        def unscale(x):
            now[x + 1] = now[x + 1] * scale[x + 1]

        rows(unscale)

    z, x, y = split(pump[0])
    spot = (z_at == z) & (y_at == y)
    rhs[x] = rhs[x] + jnp.where(spot, -PUMP_RATE * scale[x + 1], 0.0)
    solve(head_a, head_b, False)

    def clear(x):
        rhs[x] = blank

    rows(clear)

    @pl.loop(0, ports.shape[1])
    def _(port):
        z, x, y = split(ports[0, port])
        spot = (z_at == z) & (y_at == y)
        misfit = (head_a[x + 1] - heads[0, port]) * (1.0 / NOISE_VAR)
        rhs[x] = rhs[x] + jnp.where(spot, misfit * scale[x + 1], 0.0)

    solve(adj_a, adj_b, True)

    first_row = place[0]
    for row in range(slab):
        x = first_row + row
        h, a = head_a[x + 1], adj_a[x + 1]
        total = (a - adj_a[x]) * (h - head_a[x])
        total += (a - adj_a[x + 2]) * (h - head_a[x + 2])
        for move, mask in ((z_before, z_lo), (z_after, z_hi), (y_before, y_lo), (y_after, y_hi)):
            total += (a - jnp.where(mask, 0.0, move(a))) * (h - jnp.where(mask, 0.0, move(h)))
        terms[row] = -0.5 * cond[x + 1] * total
    out[...] = jnp.swapaxes(terms[...], 0, 1)


def shards(log_conductivity, storage, recharge, pump_cells, obs_cells, obs_heads):
    depth, slab, width = log_conductivity.shape
    dom_count = lax.axis_size("dom")
    dom_index = lax.axis_index("dom")
    full_x = slab * dom_count
    whole = pltpu.VMEM((full_x, depth, width), jnp.float32)
    padded = pltpu.VMEM((full_x + 2, depth, width), jnp.float32)
    smem = pl.BlockSpec(memory_space=pltpu.SMEM)
    vmem = pl.BlockSpec(memory_space=pltpu.VMEM)
    chips = dom_count // 2
    cells = pl.pallas_call(
        functools.partial(gather_kernel, dom_count),
        out_shape=jax.ShapeDtypeStruct((3, full_x, depth, width), jnp.float32),
        in_specs=[vmem] * 3,
        out_specs=vmem,
        scratch_shapes=[pltpu.SemaphoreType.DMA((chips, 3))] * 2
        + [pltpu.SemaphoreType.DMA((max(chips - 1, 1), 3))] * 2,
        compiler_params=pltpu.CompilerParams(
            collective_id=0, has_side_effects=True, vmem_limit_bytes=VMEM_LIMIT
        ),
    )(log_conductivity, storage, recharge)
    partial = pl.pallas_call(
        functools.partial(solve_kernel, slab),
        out_shape=jax.ShapeDtypeStruct((depth, slab, width), jnp.float32),
        in_specs=[smem] * 5 + [vmem],
        out_specs=vmem,
        scratch_shapes=[padded] * 3 + [whole] * 3 + [padded] * 4
        + [pltpu.VMEM((slab, depth, width), jnp.float32)],
        compiler_params=pltpu.CompilerParams(vmem_limit_bytes=VMEM_LIMIT),
    )(
        jnp.asarray(sweep_constants()),
        (dom_index * slab).astype(jnp.int32).reshape(1),
        pump_cells,
        obs_cells,
        obs_heads,
        cells,
    )
    tests = lax.axis_size("test")
    layers = depth // tests
    gradient, full = pl.pallas_call(
        functools.partial(reduce_kernel, tests, dom_count),
        out_shape=(
            jax.ShapeDtypeStruct((layers, slab, width), jnp.float32),
            jax.ShapeDtypeStruct((layers, full_x, width), jnp.float32),
        ),
        in_specs=[vmem],
        out_specs=(vmem, vmem),
        scratch_shapes=[pltpu.VMEM((tests - 1, layers, slab, width), jnp.float32)]
        + [pltpu.SemaphoreType.DMA((tests - 1,))] * 2
        + [pltpu.SemaphoreType.DMA((dom_count - 1,))] * 2,
        compiler_params=pltpu.CompilerParams(
            collective_id=1, has_side_effects=True, vmem_limit_bytes=VMEM_LIMIT
        ),
    )(partial)
    basis_x, freq_x = fourier_basis(full_x)
    basis_y, freq_y = fourier_basis(width)
    weights = jnp.asarray(prior_table(freq_x, full_x, freq_y, width), jnp.float32)
    basis_x = jnp.asarray(basis_x, jnp.float32)
    basis_y = jnp.asarray(basis_y, jnp.float32)
    spectral = jnp.dot(full.reshape(-1, width), basis_y.T, precision=lax.Precision.HIGH)
    spectral = spectral.reshape(layers, full_x, width)
    filtered = jnp.einsum("fx,mxk->mfk", basis_x, spectral, precision=HIGHEST) * weights
    own_x = lax.dynamic_slice_in_dim(basis_x, dom_index * slab, slab, axis=1)
    back = jnp.einsum("fx,mfk->mxk", own_x, filtered, precision=HIGHEST)
    step_field = jnp.dot(back.reshape(-1, width), basis_y, precision=lax.Precision.HIGH)
    return gradient, step_field.reshape(layers, slab, width)


def solution(mesh):
    in_specs = (
        P("grp", "dom", None),
        P("grp", "dom", None),
        P("grp", "dom", None),
        P(("grp", "test")),
        P(("grp", "test"), None),
        P(("grp", "test"), None),
    )
    out_specs = (P(("grp", "test"), "dom", None), P(("grp", "test"), "dom", None))
    return jax.shard_map(shards, mesh=mesh, in_specs=in_specs, out_specs=out_specs, check_vma=False)
```

```python
import functools
import math

import jax
import jax.numpy as jnp
import numpy as np
from jax import lax
from jax.experimental import pallas as pl
from jax.experimental.pallas import tpu as pltpu
from jax.sharding import PartitionSpec as P

ITERS = 32
CORR = 16
LOW = 0.1
HIGH = 2.0
PUMP_RATE = 8.0
NOISE_VAR = 0.01
NUGGET = 1.0
SMOOTH = 2.0
HIGHEST = lax.Precision.HIGHEST
UNROLL = 32
MESH = pl.DeviceIdType.MESH
VMEM_LIMIT = 56 * 1024 * 1024


def sweep_constants():
    centre = 0.5 * (HIGH + LOW)
    span = 0.5 * (HIGH - LOW)
    ratio = centre / span
    rho = 1.0 / ratio
    own, keep, step = [], [], []
    for _ in range(ITERS):
        rho_new = 1.0 / (2.0 * ratio - rho)
        keep.append(rho_new * rho)
        step.append(2.0 * rho_new / span)
        own.append(1.0 + keep[-1] - step[-1])
        rho = rho_new
    return np.array([own, keep, step], np.float32)


def fourier_basis(length):
    where = np.arange(length)
    rows, freqs = [], []
    for freq in range(length // 2 + 1):
        angle = 2.0 * np.pi / length * ((freq * where) % length)
        edge = freq == 0 or 2 * freq == length
        scale = math.sqrt((1.0 if edge else 2.0) / length)
        rows.append(scale * np.cos(angle))
        freqs.append(freq)
        if not edge:
            rows.append(scale * np.sin(angle))
            freqs.append(freq)
    return np.stack(rows), np.array(freqs, np.float64)


def prior_table(freq_x, full_x, freq_y, full_y):
    wave_x = freq_x * (2.0 * np.pi / full_x)
    wave_y = freq_y * (2.0 * np.pi / full_y)
    wave_sq = wave_x[:, None] ** 2 + wave_y[None, :] ** 2
    return NUGGET + SMOOTH * CORR**2 / (1.0 + CORR**2 * wave_sq) ** 2


def gather_kernel(
    count, conduct, storage, recharge, cells, near_send, near_recv, far_send, far_recv
):
    slab = conduct.shape[1]
    chips = count // 2
    me = lax.axis_index("dom")
    core, chip = lax.rem(me, 2), lax.div(me, 2)
    twin = me + 1 - 2 * core
    barrier = pltpu.get_barrier_semaphore()

    def far(hop):
        return 2 * lax.rem(chip + hop, chips) + core

    for peer in [twin] + [far(hop) for hop in range(1, chips)]:
        pl.semaphore_signal(barrier, 1, device_id={"dom": peer}, device_id_type=MESH)

    def block(field, owner):
        return cells.at[field, pl.ds(owner * slab, slab)]

    def near_copy(slot, field, owner):
        return pltpu.make_async_remote_copy(
            src_ref=block(field, owner),
            dst_ref=block(field, owner),
            send_sem=near_send.at[slot, field],
            recv_sem=near_recv.at[slot, field],
            device_id={"dom": twin},
            device_id_type=MESH,
        )

    def far_copy(hop, field, owner):
        return pltpu.make_async_remote_copy(
            src_ref=block(field, owner),
            dst_ref=block(field, owner),
            send_sem=far_send.at[hop - 1, field],
            recv_sem=far_recv.at[hop - 1, field],
            device_id={"dom": far(hop)},
            device_id_type=MESH,
        )

    own = pl.ds(me * slab, slab)
    for field, ref in enumerate((conduct, storage, recharge)):
        values = jnp.swapaxes(ref[...], 0, 1)
        cells[field, own] = jnp.exp(values) if field == 0 else values
        if field == 0:
            pl.semaphore_wait(barrier, chips)
        for hop in range(1, chips):
            far_copy(hop, field, me).start()
        near_copy(0, field, me).start()
    for hop in range(1, chips):
        source = far(chips - hop)
        for field in range(3):
            far_copy(hop, field, source).wait_recv()
            near_copy(hop, field, source).start()
    for field in range(3):
        for hop in range(1, chips):
            far_copy(hop, field, me).wait_send()
        for hop in range(chips):
            mine = me if hop == 0 else far(chips - hop)
            near_copy(hop, field, mine).wait_send()
            near_copy(hop, field, mine + 1 - 2 * core).wait_recv()


def reduce_kernel(
    tests, count, part, grad, full, landing, test_send, test_recv, dom_send, dom_recv
):
    layers, slab = grad.shape[:2]
    test, me = lax.axis_index("test"), lax.axis_index("dom")
    barrier = pltpu.get_barrier_semaphore()

    def test_at(hop):
        return lax.rem(test + hop, tests)

    def dom_at(hop):
        return lax.rem(me + hop, count)

    for hop in range(1, tests):
        pl.semaphore_signal(barrier, 1, device_id={"test": test_at(hop)}, device_id_type=MESH)
    for hop in range(1, count):
        pl.semaphore_signal(barrier, 1, device_id={"dom": dom_at(hop)}, device_id_type=MESH)
    pl.semaphore_wait(barrier, tests + count - 2)

    def test_copy(hop):
        return pltpu.make_async_remote_copy(
            src_ref=part.at[pl.ds(test_at(hop) * layers, layers)],
            dst_ref=landing.at[hop - 1],
            send_sem=test_send.at[hop - 1],
            recv_sem=test_recv.at[hop - 1],
            device_id={"test": test_at(hop)},
            device_id_type=MESH,
        )

    def dom_copy(hop, owner):
        place = full.at[:, pl.ds(owner * slab, slab)]
        return pltpu.make_async_remote_copy(
            src_ref=place,
            dst_ref=place,
            send_sem=dom_send.at[hop - 1],
            recv_sem=dom_recv.at[hop - 1],
            device_id={"dom": dom_at(hop)},
            device_id_type=MESH,
        )

    for hop in range(1, tests):
        test_copy(hop).start()
    total = part[pl.ds(test * layers, layers)]
    for hop in range(1, tests):
        test_copy(hop).wait_recv()
        total = total + landing[hop - 1]
    grad[...] = total
    full[:, pl.ds(me * slab, slab)] = total
    for hop in range(1, count):
        dom_copy(hop, me).start()
    for hop in range(1, tests):
        test_copy(hop).wait_send()
    for hop in range(1, count):
        dom_copy(hop, me).wait_send()
        dom_copy(hop, dom_at(count - hop)).wait_recv()


def solve_kernel(
    slab, consts, place, pump, ports, heads, cells, out,
    cond, scale, c_x, c_y, c_z, rhs, head_a, head_b, adj_a, adj_b, terms,
):
    full_x = cells.shape[1]
    depth, width = cells.shape[2:]
    z_at = lax.broadcasted_iota(jnp.int32, (depth, width), 0)
    y_at = lax.broadcasted_iota(jnp.int32, (depth, width), 1)
    z_lo, z_hi = z_at == 0, z_at == depth - 1
    y_lo, y_hi = y_at == 0, y_at == width - 1
    blank = jnp.zeros((depth, width), jnp.float32)

    def z_before(v):
        return pltpu.roll(v, 1, 0)

    def z_after(v):
        return pltpu.roll(v, depth - 1, 0)

    def y_before(v):
        return pltpu.roll(v, 1, 1)

    def y_after(v):
        return pltpu.roll(v, width - 1, 1)

    for field in (cond, scale, c_x, head_a, head_b, adj_a, adj_b):
        field[0] = blank
        field[full_x + 1] = blank

    def rows(body):
        @pl.loop(0, full_x // UNROLL)
        def _(block):
            for inner in range(UNROLL):
                body(block * UNROLL + inner)

    def fill(x):
        cond[x + 1] = cells[0, x]

    c_x[full_x] = blank
    rows(fill)
    first = 1.0 / (0.5 * (HIGH + LOW))

    def faces(x):
        here = cond[x + 1]
        f_zm = 0.5 * (here + jnp.where(z_lo, 0.0, z_before(here)))
        f_zp = 0.5 * (here + jnp.where(z_hi, 0.0, z_after(here)))
        f_xm = 0.5 * (here + cond[x])
        f_xp = 0.5 * (here + cond[x + 2])
        f_ym = 0.5 * (here + jnp.where(y_lo, 0.0, y_before(here)))
        f_yp = 0.5 * (here + jnp.where(y_hi, 0.0, y_after(here)))
        root = 1.0 / jnp.sqrt(cells[1, x] + f_zm + f_zp + f_xm + f_xp + f_ym + f_yp)
        scale[x + 1] = root
        c_x[x] = f_xm
        c_y[x] = f_yp
        c_z[x] = f_zp
        rhs[x] = cells[2, x] * root

    rows(faces)

    def couple(x):
        root = scale[x + 1]
        c_x[x] = c_x[x] * root * scale[x]
        c_y[x] = jnp.where(y_hi, 0.0, c_y[x] * root * y_after(root))
        c_z[x] = jnp.where(z_hi, 0.0, c_z[x] * root * z_after(root))

    rows(couple)

    def split(cell):
        plane = full_x * width
        rest = lax.rem(cell, plane)
        return lax.div(cell, plane), lax.div(rest, width), lax.rem(rest, width)

    def solve(now, other, near_slab):
        def start(x):
            now[x + 1] = rhs[x] * first
            other[x + 1] = blank

        rows(start)

        def sweep(src, dst, k):
            own, keep, step = consts[0, k], consts[1, k], consts[2, k]
            low, high = 0, full_x // UNROLL
            if near_slab:
                reach = ITERS - k
                low = lax.div(jnp.maximum(place[0] - reach, 0), UNROLL)
                high = lax.div(jnp.minimum(place[0] + slab + reach, full_x) + UNROLL - 1, UNROLL)

            @pl.loop(low, high)
            def _(block):
                base = block * UNROLL
                left = c_x[base] * src[base]
                here = src[base + 1]
                for inner in range(UNROLL):
                    x = base + inner
                    right = src[x + 2]
                    face_x, face_y, face_z = c_x[x + 1], c_y[x], c_z[x]
                    total = rhs[x] + left + face_x * right
                    total += face_z * z_after(here) + z_before(face_z * here)
                    total += face_y * y_after(here) + y_before(face_y * here)
                    dst[x + 1] = own * here - keep * dst[x + 1] + step * total
                    left, here = face_x * here, right

        @pl.loop(0, ITERS // 2)
        def _(pair):
            sweep(now, other, 2 * pair)
            sweep(other, now, 2 * pair + 1)

        def unscale(x):
            now[x + 1] = now[x + 1] * scale[x + 1]

        rows(unscale)

    z, x, y = split(pump[0])
    spot = (z_at == z) & (y_at == y)
    rhs[x] = rhs[x] + jnp.where(spot, -PUMP_RATE * scale[x + 1], 0.0)
    solve(head_a, head_b, False)

    def clear(x):
        rhs[x] = blank

    rows(clear)

    @pl.loop(0, ports.shape[1])
    def _(port):
        z, x, y = split(ports[0, port])
        spot = (z_at == z) & (y_at == y)
        misfit = (head_a[x + 1] - heads[0, port]) * (1.0 / NOISE_VAR)
        rhs[x] = rhs[x] + jnp.where(spot, misfit * scale[x + 1], 0.0)

    solve(adj_a, adj_b, True)

    first_row = place[0]
    for row in range(slab):
        x = first_row + row
        h, a = head_a[x + 1], adj_a[x + 1]
        total = (a - adj_a[x]) * (h - head_a[x])
        total += (a - adj_a[x + 2]) * (h - head_a[x + 2])
        for move, mask in ((z_before, z_lo), (z_after, z_hi), (y_before, y_lo), (y_after, y_hi)):
            total += (a - jnp.where(mask, 0.0, move(a))) * (h - jnp.where(mask, 0.0, move(h)))
        terms[row] = -0.5 * cond[x + 1] * total
    out[...] = jnp.swapaxes(terms[...], 0, 1)


def shards(log_conductivity, storage, recharge, pump_cells, obs_cells, obs_heads):
    depth, slab, width = log_conductivity.shape
    dom_count = lax.axis_size("dom")
    dom_index = lax.axis_index("dom")
    full_x = slab * dom_count
    whole = pltpu.VMEM((full_x, depth, width), jnp.float32)
    padded = pltpu.VMEM((full_x + 2, depth, width), jnp.float32)
    smem = pl.BlockSpec(memory_space=pltpu.SMEM)
    vmem = pl.BlockSpec(memory_space=pltpu.VMEM)
    chips = dom_count // 2
    cells = pl.pallas_call(
        functools.partial(gather_kernel, dom_count),
        out_shape=jax.ShapeDtypeStruct((3, full_x, depth, width), jnp.float32),
        in_specs=[vmem] * 3,
        out_specs=vmem,
        scratch_shapes=[pltpu.SemaphoreType.DMA((chips, 3))] * 2
        + [pltpu.SemaphoreType.DMA((max(chips - 1, 1), 3))] * 2,
        compiler_params=pltpu.CompilerParams(
            collective_id=0, has_side_effects=True, vmem_limit_bytes=VMEM_LIMIT
        ),
    )(log_conductivity, storage, recharge)
    partial = pl.pallas_call(
        functools.partial(solve_kernel, slab),
        out_shape=jax.ShapeDtypeStruct((depth, slab, width), jnp.float32),
        in_specs=[smem] * 5 + [vmem],
        out_specs=vmem,
        scratch_shapes=[padded] * 3 + [whole] * 3 + [padded] * 4
        + [pltpu.VMEM((slab, depth, width), jnp.float32)],
        compiler_params=pltpu.CompilerParams(vmem_limit_bytes=VMEM_LIMIT),
    )(
        jnp.asarray(sweep_constants()),
        (dom_index * slab).astype(jnp.int32).reshape(1),
        pump_cells,
        obs_cells,
        obs_heads,
        cells,
    )
    tests = lax.axis_size("test")
    layers = depth // tests
    gradient, full = pl.pallas_call(
        functools.partial(reduce_kernel, tests, dom_count),
        out_shape=(
            jax.ShapeDtypeStruct((layers, slab, width), jnp.float32),
            jax.ShapeDtypeStruct((layers, full_x, width), jnp.float32),
        ),
        in_specs=[vmem],
        out_specs=(vmem, vmem),
        scratch_shapes=[pltpu.VMEM((tests - 1, layers, slab, width), jnp.float32)]
        + [pltpu.SemaphoreType.DMA((tests - 1,))] * 2
        + [pltpu.SemaphoreType.DMA((dom_count - 1,))] * 2,
        compiler_params=pltpu.CompilerParams(
            collective_id=1, has_side_effects=True, vmem_limit_bytes=VMEM_LIMIT
        ),
    )(partial)
    basis_x, freq_x = fourier_basis(full_x)
    basis_y, freq_y = fourier_basis(width)
    weights = jnp.asarray(prior_table(freq_x, full_x, freq_y, width), jnp.float32)
    basis_x = jnp.asarray(basis_x, jnp.float32)
    basis_y = jnp.asarray(basis_y, jnp.float32)
    spectral = jnp.dot(full.reshape(-1, width), basis_y.T, precision=lax.Precision.HIGH)
    spectral = spectral.reshape(layers, full_x, width)
    filtered = jnp.einsum("fx,mxk->mfk", basis_x, spectral, precision=HIGHEST) * weights
    own_x = lax.dynamic_slice_in_dim(basis_x, dom_index * slab, slab, axis=1)
    back = jnp.einsum("fx,mfk->mxk", own_x, filtered, precision=HIGHEST)
    step_field = jnp.dot(back.reshape(-1, width), basis_y, precision=lax.Precision.HIGH)
    return gradient, step_field.reshape(layers, slab, width)


def solution(mesh):
    in_specs = (
        P("grp", "dom", None),
        P("grp", "dom", None),
        P("grp", "dom", None),
        P(("grp", "test")),
        P(("grp", "test"), None),
        P(("grp", "test"), None),
    )
    out_specs = (P(("grp", "test"), "dom", None), P(("grp", "test"), "dom", None))
    return jax.shard_map(shards, mesh=mesh, in_specs=in_specs, out_specs=out_specs, check_vma=False)
```
